128 devices in a mesh: row: 32 (over x, z, core), rep: 4 (over y).
Axes of the slice: x: 4, y: 4, z: 4, core: 2. Of those that a mesh axis runs over, the one named last changes fastest.
Arguments:
- features: bfloat16 [32768, 512], P('row'), may hold values from -6 to 6
- block_index: int32 [256, 192], P('row', 'rep'), may hold values from 0 to 255, as said below
- counts: int32 [256], P('row'), may hold values from 48 to 192, as said below
- values: bfloat16 [256, 192, 128, 128], P('row', 'rep'), may hold values from -0.0546875 to 0.0546875
- weight: bfloat16 [512, 512], replicated, may hold values from -0.25 to 0.25
- bias: float32 [512], replicated, may hold values from -1 to 1
- cotangent: bfloat16 [32768, 512], P(('row', 'rep')), may hold values from -6 to 6
Outputs:
- output: bfloat16 [32768, 512], P(('row', 'rep'))
- weight_grad: float32 [512, 512], replicated
- bias_grad: float32 [512], replicated
The draws below stay inside these ranges and needn't reach their ends.
Inputs may be any that keep to these rules, and one draw needn't show every extreme that they name: `block_index`: A slot s of a row block names a column block c with c % 4 == s // 48; block 0 and block 255 are named. `counts`: some row block has all 192 slots live.
All inputs are finite; a program needn't handle non-finite values.
Results may differ from the reference program's by a relative error of at most 0.0056.
Values may be sent and summed in bfloat16 or wider, within the bound.
No kernel may reach another device: no remote copies, remote signals or barrier semaphores. Data moves between devices by JAX's collectives and lax.ppermute only.
A program may use at most 128 MiB of HBM per device.

```python
import jax
import jax.numpy as jnp
from jax import lax

F = 512
ROWB = 128
S = 192
NBLK = 256
NODES = 32768
N_REP = 4


def draw_block_index(key, part):
    key = jax.random.fold_in(key, 11)
    member = jnp.arange(S, dtype=jnp.int32) // (S // N_REP)
    picks = jax.random.randint(key, (NBLK, S), 0, NBLK // N_REP)
    names = picks * N_REP + member[None, :]
    names = names.at[0, 0].set(0)
    names = names.at[0, S - 1].set(NBLK - 1)
    return names.astype(jnp.int32)


def draw_counts(key, part):
    key = jax.random.fold_in(key, 23)
    drawn = jax.random.randint(key, (NBLK,), S // 4, S + 1)
    return drawn.at[0].set(S).astype(jnp.int32)


def shard_levels(key, shape, shards, low, top_value):
    def one(position, blocks):
        steps = jax.random.uniform(jax.random.fold_in(jax.random.fold_in(key, 6), position), (blocks,), jnp.float32, low / len(shards), top_value / len(shards))
        return jnp.repeat(jnp.exp(steps), shape[position] // blocks).reshape((-1,) + (1,) * (len(shape) - position - 1))

    loudness = one(*shards[0])
    for cut in shards[1:]:
        loudness = loudness * one(*cut)
    return loudness


def noise(stream_key, dims, scale, reach, shards=(), held_as=jnp.bfloat16):
    gain = shard_levels(stream_key, dims, shards, -0.22, 0.18) if shards else 1.0
    array = jax.random.normal(stream_key, dims, jnp.float32) * scale * gain
    return jnp.minimum(jnp.maximum(array, -reach), reach).astype(held_as)


def setup_inputs(seed: int = 0) -> dict:
    key_of = jax.random.split(jax.random.key(seed), 8)
    features = noise(key_of[0], (NODES, F), 1.0, 6.0, ((0, 32),))
    block_index = draw_block_index(jax.random.fold_in(key_of[7], 71), 0)
    counts = draw_counts(jax.random.fold_in(key_of[7], 71), 0)
    values = noise(key_of[3], (NBLK, S, ROWB, ROWB), (S * ROWB // 2) ** -0.5, 0.0546875, ((0, 32), (1, 4)))
    weight = noise(key_of[4], (F, F), F ** -0.5, 0.25)
    bias = jnp.clip(jax.random.uniform(key_of[5], (F,), jnp.float32, -1.0, 1.0), -1.0, 1.0)
    cotangent = noise(key_of[6], (NODES, F), 1.0, 6.0, ((0, 128),))
    return {"features": features, "block_index": block_index, "counts": counts, "values": values, "weight": weight, "bias": bias, "cotangent": cotangent}


def reference(features, block_index, counts, values, weight, bias, cotangent):
    blocks = features.reshape(NBLK, ROWB, F)
    slot_ids = jnp.arange(S, dtype=jnp.int32)

    def one_block(packed):
        names, count, vals = packed
        picked = blocks[names].astype(jnp.float32)
        live = (slot_ids < count).astype(jnp.float32)
        scaled = vals.astype(jnp.float32) * live[:, None, None]
        return jnp.einsum("smn,snf->mf", scaled, picked)

    summed = lax.map(one_block, (block_index, counts, values))
    aggregated = summed.reshape(NODES, F).astype(jnp.bfloat16)
    pre = jnp.dot(aggregated, weight, preferred_element_type=jnp.float32) + bias
    output = (pre * jax.nn.sigmoid(pre)).astype(jnp.bfloat16)
    sig = jax.nn.sigmoid(pre)
    delta_f = cotangent.astype(jnp.float32) * sig * (1.0 + pre * (1.0 - sig))
    delta = delta_f.astype(jnp.bfloat16)
    weight_grad = jnp.dot(aggregated.T, delta, preferred_element_type=jnp.float32)
    bias_grad = jnp.sum(delta_f, axis=0)
    return output, weight_grad, bias_grad
```

```python
import jax
import jax.numpy as jnp
from jax import lax
from jax.experimental import pallas as pl
from jax.experimental.pallas import tpu as pltpu
from jax.sharding import PartitionSpec as P

NCHUNK = 1
BF16 = jnp.bfloat16
F32 = jnp.float32
N_ROW = 32
N_REP = 4
OFFSETS = (0, -1, 1, 2)


def _row(x, z, c):
    return (x % 4) * 8 + (z % 4) * 2 + c


def _axis_perm(first, step):
    pairs = []
    for x in range(4):
        for z in range(4):
            for c in range(2):
                along_x = (c == 0) == first
                dst = _row(x + step, z, c) if along_x else _row(x, z + step, c)
                pairs.append((_row(x, z, c), dst))
    return pairs


SWAP = [(r, r ^ 1) for r in range(N_ROW)]


def _send(x, first, step):
    return lax.ppermute(x, "row", _axis_perm(first, step))


def _swap(x):
    return lax.ppermute(x, "row", SWAP)


def _rep_send(x, k):
    return lax.ppermute(x, "rep", [(i, (i + k) % N_REP) for i in range(N_REP)])


def gather_pieces(mine):
    from_lo = _send(mine, True, 1)
    from_hi = _send(mine, True, -1)
    from_far = _send(mine, True, 2)
    own = jnp.concatenate([mine, from_lo, from_hi, from_far], axis=0)
    half = own.shape[0] // 2
    lo = _send(own, False, 1)
    hi = _send(own, False, -1)
    far_a = _send(lo[:half], False, 1)
    far_b = _send(hi[half:], False, -1)
    pieces = [own, lo, hi, far_a, far_b]
    return pieces + [_swap(p) for p in pieces]


def table_index(block_index, live):
    me = lax.axis_index("row")
    x, z, c = me // 8, (me // 2) % 4, me % 2
    r = block_index // 8
    dx = (r // 8 - x) % 4
    dz = ((r // 2) % 4 - z) % 4
    cs = r % 2
    rank = lambda d: jnp.where(d == 0, 0, jnp.where(d == 3, 1, jnp.where(d == 1, 2, 3)))
    kx, kz = rank(dx), rank(dz)
    k1 = jnp.where(cs == 0, kx, kz)
    k2 = jnp.where(cs == 0, kz, kx)
    other = (cs != c).astype(jnp.int32)
    pos = ((other * 4 + k2) * 4 + k1) * 2 + (block_index // 4) % 2
    slot = jnp.arange(block_index.shape[1], dtype=jnp.int32)
    return jnp.where(slot < live[:, None], pos, 2 * N_ROW).astype(jnp.int32)


def spmm(index, values, pieces, member):
    rb, s, rowb, _ = values.shape
    width = pieces[0].shape[1]
    n_p = len(pieces)
    blocks = [p.shape[0] // rowb for p in pieces]
    total = sum(blocks)
    per = rb // N_REP

    def kernel(m_ref, idx_ref, v_hbm, *rest):
        p_hbm = rest[:n_p]
        outs = rest[n_p : n_p + N_REP]
        t_ref, v_ref, t_sem, v_sem = rest[n_p + N_REP :]
        m = m_ref[0]

        def source(i):
            return lax.rem(m + i // per, N_REP) * per + i % per

        t_copies, at = [], 0
        for i in range(n_p):
            t_copies.append(
                pltpu.make_async_copy(p_hbm[i], t_ref.at[pl.ds(at * rowb, blocks[i] * rowb)], t_sem.at[i])
            )
            at += blocks[i]
        v_copies = [pltpu.make_async_copy(v_hbm.at[source(i)], v_ref.at[i], v_sem.at[i]) for i in range(rb)]
        for cp in t_copies + v_copies:
            cp.start()
        t_ref[pl.ds(total * rowb, rowb), :] = jnp.zeros((rowb, width), BF16)
        for cp in t_copies:
            cp.wait()
        for i in range(rb):
            v_copies[i].wait()
            b = source(i)
            acc = jnp.zeros((rowb, width), F32)
            for p in range(s // 2):
                lhs = jnp.concatenate([v_ref[i, 2 * p], v_ref[i, 2 * p + 1]], axis=1)
                rows = [
                    t_ref[pl.ds(pl.multiple_of(idx_ref[b, 2 * p + q] * rowb, rowb), rowb), :]
                    for q in range(2)
                ]
                rhs = jnp.concatenate(rows, axis=0)
                acc = acc + jnp.dot(lhs, rhs, preferred_element_type=F32)
            outs[i // per][pl.ds((i % per) * rowb, rowb), :] = acc.astype(BF16)

    flops = 2 * rb * s * rowb * rowb * width
    nbytes = values.size * 2 + total * rowb * width * 2
    return pl.pallas_call(
        kernel,
        in_specs=[pl.BlockSpec(memory_space=pltpu.SMEM)] * 2 + [pl.BlockSpec(memory_space=pl.ANY)] * (1 + n_p),
        out_specs=[pl.BlockSpec(memory_space=pltpu.VMEM)] * N_REP,
        out_shape=[jax.ShapeDtypeStruct((per * rowb, width), BF16)] * N_REP,
        scratch_shapes=[
            pltpu.VMEM(((total + 1) * rowb, width), BF16),
            pltpu.VMEM(values.shape, BF16),
            pltpu.SemaphoreType.DMA((n_p,)),
            pltpu.SemaphoreType.DMA((rb,)),
        ],
        compiler_params=pltpu.CompilerParams(vmem_limit_bytes=40 << 20),
        cost_estimate=pl.CostEstimate(flops=flops, bytes_accessed=nbytes, transcendentals=0),
    )(member, index, values, *pieces)


def tail(parts, weight, bias, cotangent):
    nodes, width = cotangent.shape
    n_c = len(parts)
    flat = [p for chunk in parts for p in chunk]

    def kernel(*refs):
        part_refs = refs[: len(flat)]
        w_ref, b_ref, g_ref, out_ref, grad_ref = refs[len(flat) :]
        agg = []
        pre = jnp.zeros((nodes, width), F32)
        for c in range(n_c):
            group = part_refs[c * N_REP : (c + 1) * N_REP]
            a = group[0][...].astype(F32)
            for r in group[1:]:
                a = a + r[...].astype(F32)
            a = a.astype(BF16)
            agg.append(a)
            w = a.shape[1]
            pre = pre + jnp.dot(a, w_ref[pl.ds(c * w, w), :], preferred_element_type=F32)
        pre = pre + b_ref[...]
        sig = jax.nn.sigmoid(pre)
        out_ref[...] = (pre * sig).astype(BF16)
        delta_f = g_ref[...].astype(F32) * sig * (1.0 + pre * (1.0 - sig))
        delta = delta_f.astype(BF16)
        grad_ref[...] = jnp.zeros(grad_ref.shape, BF16)
        bias_row = jnp.sum(delta_f, axis=0, keepdims=True)
        for k in range(4):
            grad_ref[k, pl.ds(16, 8), :] = jnp.broadcast_to(
                bias_row[:, k * 128 : (k + 1) * 128] * 0.125, (8, 128)
            ).astype(BF16)
        for c in range(n_c):
            a = agg[c]
            w = a.shape[1]
            g = lax.dot_general(a, delta, (((0,), (0,)), ((), ())), preferred_element_type=F32).astype(BF16)
            for r in range(w // 16):
                for k in range(4):
                    grad_ref[((c * w) // 16 + r) * 4 + k, pl.ds(0, 16), :] = g[
                        r * 16 : (r + 1) * 16, k * 128 : (k + 1) * 128
                    ]

    return pl.pallas_call(
        kernel,
        out_shape=[
            jax.ShapeDtypeStruct((nodes, width), BF16),
            jax.ShapeDtypeStruct((128, 32, 128), BF16),
        ],
        compiler_params=pltpu.CompilerParams(vmem_limit_bytes=32 << 20),
    )(*flat, weight, bias.reshape(1, -1), cotangent)


def per_device(features, block_index, counts, values, weight, bias, cotangent):
    rb, s = block_index.shape
    rowb = values.shape[2]
    width = features.shape[1]
    member = lax.axis_index("rep")
    live = jnp.clip(counts - member * s, 0, s)
    index = table_index(block_index, live)
    mine = lax.dynamic_index_in_dim(features.reshape(2, N_REP, rowb, width), member, 1, False)
    mine = mine.reshape(2 * rowb, width)
    m_arr = member.astype(jnp.int32).reshape(1)
    w = width // NCHUNK
    parts = []
    for c in range(NCHUNK):
        pieces = gather_pieces(mine[:, c * w : (c + 1) * w])
        sums = spmm(index, values, pieces, m_arr)
        parts.append([sums[0]] + [_rep_send(sums[k], k) for k in range(1, N_REP)])
    output, packed = tail(parts, weight, bias, cotangent)
    packed = packed[:, :24]
    got = lax.all_to_all(packed, ("row", "rep"), 0, 0, tiled=False)
    mysum = jnp.sum(got.astype(F32), axis=0).astype(BF16)
    back = lax.all_to_all(jnp.broadcast_to(mysum[None], packed.shape), ("row", "rep"), 0, 0, tiled=False)
    weight_grad = (
        back[:, :16].reshape(32, 4, 16, 128).transpose(0, 2, 1, 3).reshape(width, width).astype(F32)
    )
    bias_grad = jnp.sum(back[:4, 16:24].astype(F32), axis=1).reshape(width)
    return (output, weight_grad, bias_grad)


def solution(mesh):
    return jax.shard_map(
        per_device,
        mesh=mesh,
        in_specs=(
            P("row", None),
            P("row", "rep"),
            P("row"),
            P("row", "rep", None, None),
            P(),
            P(),
            P(("row", "rep"), None),
        ),
        out_specs=(P(("row", "rep"), None), P(), P()),
        check_vma=False,
    )
```

```python
import jax
import jax.numpy as jnp
from jax import lax
from jax.experimental import pallas as pl
from jax.experimental.pallas import tpu as pltpu
from jax.sharding import PartitionSpec as P

BF16 = jnp.bfloat16
F32 = jnp.float32
N_ROW = 32
N_REP = 4
OFFSETS = (1, -1, 2)


def _row(x, z, c):
    return (x % 4) * 8 + (z % 4) * 2 + c


def _axis_perm(first, step):
    pairs = []
    for x in range(4):
        for z in range(4):
            for c in range(2):
                along_x = (c == 0) == first
                dst = _row(x + step, z, c) if along_x else _row(x, z + step, c)
                pairs.append((_row(x, z, c), dst))
    return pairs


SWAP = [(r, r ^ 1) for r in range(N_ROW)]


def _send(x, first, step):
    return lax.ppermute(x, "row", _axis_perm(first, step))


def _swap(x):
    return lax.ppermute(x, "row", SWAP)


def _rep_send(x, k):
    return lax.ppermute(x, "rep", [(i, (i + k) % N_REP) for i in range(N_REP)])


def gather_table(mine):
    line = jnp.concatenate([mine] + [_send(mine, True, k) for k in OFFSETS], axis=0)
    pieces = [line] + [_send(line, False, k) for k in OFFSETS]
    zeros = jnp.zeros((mine.shape[0] // 2, mine.shape[1]), mine.dtype)
    return jnp.concatenate(pieces + [_swap(p) for p in pieces] + [zeros], axis=0)


def table_index(block_index, live):
    me = lax.axis_index("row")
    x, z, c = me // 8, (me // 2) % 4, me % 2
    r = block_index // 8
    dx = (r // 8 - x) % 4
    dz = ((r // 2) % 4 - z) % 4
    cs = r % 2
    rank = lambda d: jnp.where(d == 0, 0, jnp.where(d == 3, 1, jnp.where(d == 1, 2, 3)))
    kx, kz = rank(dx), rank(dz)
    k1 = jnp.where(cs == 0, kx, kz)
    k2 = jnp.where(cs == 0, kz, kx)
    other = (cs != c).astype(jnp.int32)
    pos = ((other * 4 + k2) * 4 + k1) * 2 + (block_index // 4) % 2
    slot = jnp.arange(block_index.shape[1], dtype=jnp.int32)
    return jnp.where(slot < live[:, None], pos, 2 * N_ROW).astype(jnp.int32)


def spmm(index, values, table, member, targets, received=()):
    rb, s, rowb, _ = values.shape
    width = table.shape[1]
    per = rb // N_REP
    n = per * len(targets)

    def kernel(m_ref, idx_ref, v_ref, t_ref, *rest):
        got, outs = rest[: len(received)], rest[len(received) :]
        m = m_ref[0]
        source = [lax.rem(m + targets[i // per], N_REP) * per + i % per for i in range(n)]
        for i in range(n):
            b = source[i]
            acc = jnp.zeros((rowb, width), F32)
            for p in range(0, s, 2):
                lhs = jnp.concatenate([v_ref[b, p], v_ref[b, p + 1]], axis=1)
                rows = [
                    t_ref[pl.ds(pl.multiple_of(idx_ref[b, p + q] * rowb, rowb), rowb), :] for q in range(2)
                ]
                rhs = jnp.concatenate(rows, axis=0)
                acc = acc + jnp.dot(lhs, rhs, preferred_element_type=F32)
            out = outs[i // per]
            rows = pl.ds((i % per) * rowb, rowb)
            if i < per:
                for r in got:
                    acc = acc + r[rows, :].astype(F32)
            out[rows, :] = acc.astype(out.dtype)

    return pl.pallas_call(
        kernel,
        in_specs=[
            pl.BlockSpec(memory_space=pltpu.SMEM),
            pl.BlockSpec(memory_space=pltpu.SMEM),
            pl.BlockSpec(memory_space=pltpu.VMEM),
            pl.BlockSpec(memory_space=pltpu.VMEM),
        ]
        + [pl.BlockSpec(memory_space=pltpu.VMEM)] * len(received),
        out_specs=[pl.BlockSpec(memory_space=pltpu.VMEM)] * len(targets),
        out_shape=[jax.ShapeDtypeStruct((per * rowb, width), F32 if k == 0 else BF16) for k in targets],
        compiler_params=pltpu.CompilerParams(vmem_limit_bytes=4 << 20),
        cost_estimate=pl.CostEstimate(
            flops=n * s * rowb * rowb * width // 8, bytes_accessed=n * rowb * width * 2, transcendentals=0
        ),
    )(member, index, values, table, *received)


def tail(parts, weight, bias, cotangent):
    nodes, width = cotangent.shape

    def kernel(*refs):
        part_refs = refs[: len(parts)]
        w_ref, b_ref, g_ref, out_ref, grad_ref = refs[len(parts) :]
        a = part_refs[0][...].astype(F32)
        for r in part_refs[1:]:
            a = a + r[...].astype(F32)
        a = a.astype(BF16)
        pre = jnp.dot(a, w_ref[...], preferred_element_type=F32)
        pre = pre + b_ref[...]
        sig = jax.nn.sigmoid(pre)
        out_ref[...] = (pre * sig).astype(BF16)
        delta_f = g_ref[...].astype(F32) * sig * (1.0 + pre * (1.0 - sig))
        delta = delta_f.astype(BF16)
        grad_ref[...] = jnp.zeros(grad_ref.shape, BF16)
        bias_row = jnp.sum(delta_f, axis=0, keepdims=True)
        for k in range(4):
            grad_ref[k, pl.ds(16, 8), :] = jnp.broadcast_to(
                bias_row[:, k * 128 : (k + 1) * 128] * 0.125, (8, 128)
            ).astype(BF16)
        g = lax.dot_general(a, delta, (((0,), (0,)), ((), ())), preferred_element_type=F32).astype(BF16)
        for r in range(width // 16):
            for k in range(4):
                grad_ref[r * 4 + k, pl.ds(0, 16), :] = g[r * 16 : (r + 1) * 16, k * 128 : (k + 1) * 128]

    return pl.pallas_call(
        kernel,
        out_shape=[
            jax.ShapeDtypeStruct((nodes, width), BF16),
            jax.ShapeDtypeStruct((128, 24, 128), BF16),
        ],
        compiler_params=pltpu.CompilerParams(vmem_limit_bytes=16 << 20),
    )(*parts, weight, bias.reshape(1, -1), cotangent)


def unpack(packed):
    width = 512

    def kernel(p_ref, grad_ref, bias_ref):
        for r in range(width // 16):
            for k in range(4):
                grad_ref[pl.ds(r * 16, 16), pl.ds(k * 128, 128)] = p_ref[4 * r + k, pl.ds(0, 16), :].astype(F32)
        for k in range(4):
            rows = p_ref[k, pl.ds(16, 8), :].astype(F32)
            bias_ref[:, pl.ds(k * 128, 128)] = jnp.sum(rows, axis=0, keepdims=True)

    return pl.pallas_call(
        kernel,
        out_shape=[jax.ShapeDtypeStruct((width, width), F32), jax.ShapeDtypeStruct((1, width), F32)],
        compiler_params=pltpu.CompilerParams(vmem_limit_bytes=16 << 20),
    )(packed)


def per_device(features, block_index, counts, values, weight, bias, cotangent):
    rb, s = block_index.shape
    rowb = values.shape[2]
    width = features.shape[1]
    member = lax.axis_index("rep")
    live = jnp.clip(counts - member * s, 0, s)
    index = table_index(block_index, live)
    mine = lax.dynamic_index_in_dim(features.reshape(2, N_REP, rowb, width), member, 1, False)
    mine = mine.reshape(2 * rowb, width)
    m_arr = member.astype(jnp.int32).reshape(1)
    table = gather_table(mine)
    (far,) = spmm(index, values, table, m_arr, (2,))
    far = _rep_send(far, 2)
    ahead, behind = spmm(index, values, table, m_arr, (1, 3))
    ahead, behind = _rep_send(ahead, 1), _rep_send(behind, 3)
    (own,) = spmm(index, values, table, m_arr, (0,), (far,))
    parts = [own, ahead, behind]
    output, packed = tail(parts, weight, bias, cotangent)
    got = lax.all_to_all(packed, ("row", "rep"), 0, 0, tiled=False)
    mysum = jnp.sum(got.astype(F32), axis=0).astype(BF16)
    back = lax.all_to_all(jnp.broadcast_to(mysum[None], packed.shape), ("row", "rep"), 0, 0, tiled=False)
    weight_grad, bias_grad = unpack(back)
    bias_grad = bias_grad.reshape(width)
    return (output, weight_grad, bias_grad)


def solution(mesh):
    return jax.shard_map(
        per_device,
        mesh=mesh,
        in_specs=(
            P("row", None),
            P("row", "rep"),
            P("row"),
            P("row", "rep", None, None),
            P(),
            P(),
            P(("row", "rep"), None),
        ),
        out_specs=(P(("row", "rep"), None), P(), P()),
        check_vma=False,
    )
```

```python
import jax
import jax.numpy as jnp
from jax import lax
from jax.experimental import pallas as pl
from jax.experimental.pallas import tpu as pltpu
from jax.sharding import PartitionSpec as P

BF16 = jnp.bfloat16
F32 = jnp.float32
N_ROW = 32
N_REP = 4
OFFSETS = (1, -1, 2)


def _row(x, z, c):
    return (x % 4) * 8 + (z % 4) * 2 + c


def _axis_perm(first, step):
    pairs = []
    for x in range(4):
        for z in range(4):
            for c in range(2):
                along_x = (c == 0) == first
                dst = _row(x + step, z, c) if along_x else _row(x, z + step, c)
                pairs.append((_row(x, z, c), dst))
    return pairs


SWAP = [(r, r ^ 1) for r in range(N_ROW)]


def _send(x, first, step):
    return lax.ppermute(x, "row", _axis_perm(first, step))


def _swap(x):
    return lax.ppermute(x, "row", SWAP)


def _rep_send(x, k):
    return lax.ppermute(x, "rep", [(i, (i + k) % N_REP) for i in range(N_REP)])


def gather_table(mine):
    line = jnp.concatenate([mine] + [_send(mine, True, k) for k in OFFSETS], axis=0)
    pieces = [line] + [_send(line, False, k) for k in OFFSETS]
    zeros = jnp.zeros((mine.shape[0] // 2, mine.shape[1]), mine.dtype)
    return jnp.concatenate(pieces + [_swap(p) for p in pieces] + [zeros], axis=0)


def table_index(block_index, live):
    me = lax.axis_index("row")
    x, z, c = me // 8, (me // 2) % 4, me % 2
    r = block_index // 8
    dx = (r // 8 - x) % 4
    dz = ((r // 2) % 4 - z) % 4
    cs = r % 2
    rank = lambda d: jnp.where(d == 0, 0, jnp.where(d == 3, 1, jnp.where(d == 1, 2, 3)))
    kx, kz = rank(dx), rank(dz)
    k1 = jnp.where(cs == 0, kx, kz)
    k2 = jnp.where(cs == 0, kz, kx)
    other = (cs != c).astype(jnp.int32)
    pos = ((other * 4 + k2) * 4 + k1) * 2 + (block_index // 4) % 2
    slot = jnp.arange(block_index.shape[1], dtype=jnp.int32)
    return jnp.where(slot < live[:, None], pos, 2 * N_ROW).astype(jnp.int32)


def spmm(index, values, table, member, targets, received=()):
    rb, s, rowb, _ = values.shape
    width = table.shape[1]
    per = rb // N_REP
    n = per * len(targets)

    def kernel(m_ref, idx_ref, v_ref, t_ref, *rest):
        got, outs = rest[: len(received)], rest[len(received) :]
        m = m_ref[0]
        source = [lax.rem(m + targets[i // per], N_REP) * per + i % per for i in range(n)]
        for i in range(n):
            b = source[i]
            acc = jnp.zeros((rowb, width), F32)
            for p in range(0, s, 2):
                lhs = jnp.concatenate([v_ref[b, p], v_ref[b, p + 1]], axis=1)
                rows = [
                    t_ref[pl.ds(pl.multiple_of(idx_ref[b, p + q] * rowb, rowb), rowb), :] for q in range(2)
                ]
                rhs = jnp.concatenate(rows, axis=0)
                acc = acc + jnp.dot(lhs, rhs, preferred_element_type=F32)
            out = outs[i // per]
            rows = pl.ds((i % per) * rowb, rowb)
            if i < per:
                for r in got:
                    acc = acc + r[rows, :].astype(F32)
            out[rows, :] = acc.astype(out.dtype)

    return pl.pallas_call(
        kernel,
        in_specs=[
            pl.BlockSpec(memory_space=pltpu.SMEM),
            pl.BlockSpec(memory_space=pltpu.SMEM),
            pl.BlockSpec(memory_space=pltpu.VMEM),
            pl.BlockSpec(memory_space=pltpu.VMEM),
        ]
        + [pl.BlockSpec(memory_space=pltpu.VMEM)] * len(received),
        out_specs=[pl.BlockSpec(memory_space=pltpu.VMEM)] * len(targets),
        out_shape=[jax.ShapeDtypeStruct((per * rowb, width), F32 if k == 0 else BF16) for k in targets],
        compiler_params=pltpu.CompilerParams(vmem_limit_bytes=24 << 20),
        cost_estimate=pl.CostEstimate(
            flops=n * s * rowb * rowb * width // 8, bytes_accessed=n * rowb * width * 2, transcendentals=0
        ),
    )(member, index, values, table, *received)


def tail(parts, weight, bias, cotangent):
    nodes, width = cotangent.shape

    def kernel(*refs):
        part_refs = refs[: len(parts)]
        w_ref, b_ref, g_ref, out_ref, grad_ref = refs[len(parts) :]
        a = part_refs[0][...].astype(F32)
        for r in part_refs[1:]:
            a = a + r[...].astype(F32)
        a = a.astype(BF16)
        pre = jnp.dot(a, w_ref[...], preferred_element_type=F32)
        pre = pre + b_ref[...]
        sig = jax.nn.sigmoid(pre)
        out_ref[...] = (pre * sig).astype(BF16)
        delta_f = g_ref[...].astype(F32) * sig * (1.0 + pre * (1.0 - sig))
        delta = delta_f.astype(BF16)
        grad_ref[...] = jnp.zeros(grad_ref.shape, BF16)
        bias_row = jnp.sum(delta_f, axis=0, keepdims=True)
        for k in range(4):
            grad_ref[k, pl.ds(16, 8), :] = jnp.broadcast_to(
                bias_row[:, k * 128 : (k + 1) * 128] * 0.125, (8, 128)
            ).astype(BF16)
        g = lax.dot_general(a, delta, (((0,), (0,)), ((), ())), preferred_element_type=F32).astype(BF16)
        for r in range(width // 16):
            for k in range(4):
                grad_ref[r * 4 + k, pl.ds(0, 16), :] = g[r * 16 : (r + 1) * 16, k * 128 : (k + 1) * 128]

    return pl.pallas_call(
        kernel,
        out_shape=[
            jax.ShapeDtypeStruct((nodes, width), BF16),
            jax.ShapeDtypeStruct((128, 24, 128), BF16),
        ],
        compiler_params=pltpu.CompilerParams(vmem_limit_bytes=16 << 20),
    )(*parts, weight, bias.reshape(1, -1), cotangent)


def unpack(packed):
    width = 512

    def kernel(p_ref, grad_ref, bias_ref):
        for r in range(width // 16):
            for k in range(4):
                grad_ref[pl.ds(r * 16, 16), pl.ds(k * 128, 128)] = p_ref[4 * r + k, pl.ds(0, 16), :].astype(F32)
        for k in range(4):
            rows = p_ref[k, pl.ds(16, 8), :].astype(F32)
            bias_ref[:, pl.ds(k * 128, 128)] = jnp.sum(rows, axis=0, keepdims=True)

    return pl.pallas_call(
        kernel,
        out_shape=[jax.ShapeDtypeStruct((width, width), F32), jax.ShapeDtypeStruct((1, width), F32)],
        compiler_params=pltpu.CompilerParams(vmem_limit_bytes=16 << 20),
    )(packed)


def per_device(features, block_index, counts, values, weight, bias, cotangent):
    rb, s = block_index.shape
    rowb = values.shape[2]
    width = features.shape[1]
    member = lax.axis_index("rep")
    live = jnp.clip(counts - member * s, 0, s)
    index = table_index(block_index, live)
    mine = lax.dynamic_index_in_dim(features.reshape(2, N_REP, rowb, width), member, 1, False)
    mine = mine.reshape(2 * rowb, width)
    m_arr = member.astype(jnp.int32).reshape(1)
    table = gather_table(mine)
    (far,) = spmm(index, values, table, m_arr, (2,))
    far = _rep_send(far, 2)
    ahead, behind = spmm(index, values, table, m_arr, (1, 3))
    ahead, behind = _rep_send(ahead, 1), _rep_send(behind, 3)
    (own,) = spmm(index, values, table, m_arr, (0,), (far,))
    parts = [own, ahead, behind]
    output, packed = tail(parts, weight, bias, cotangent)
    got = lax.all_to_all(packed, ("row", "rep"), 0, 0, tiled=False)
    mysum = jnp.sum(got.astype(F32), axis=0).astype(BF16)
    back = lax.all_to_all(jnp.broadcast_to(mysum[None], packed.shape), ("row", "rep"), 0, 0, tiled=False)
    weight_grad, bias_grad = unpack(back)
    bias_grad = bias_grad.reshape(width)
    return (output, weight_grad, bias_grad)


def solution(mesh):
    return jax.shard_map(
        per_device,
        mesh=mesh,
        in_specs=(
            P("row", None),
            P("row", "rep"),
            P("row"),
            P("row", "rep", None, None),
            P(),
            P(),
            P(("row", "rep"), None),
        ),
        out_specs=(P(("row", "rep"), None), P(), P()),
        check_vma=False,
    )
```

```python
import jax
import jax.numpy as jnp
from jax import lax
from jax.experimental import pallas as pl
from jax.experimental.pallas import tpu as pltpu
from jax.sharding import PartitionSpec as P

BF16 = jnp.bfloat16
F32 = jnp.float32
N_ROW = 32
N_REP = 4
OFFSETS = (1, -1, 2)


def _row(x, z, c):
    return (x % 4) * 8 + (z % 4) * 2 + c


def _axis_perm(first, step):
    pairs = []
    for x in range(4):
        for z in range(4):
            for c in range(2):
                along_x = (c == 0) == first
                dst = _row(x + step, z, c) if along_x else _row(x, z + step, c)
                pairs.append((_row(x, z, c), dst))
    return pairs


SWAP = [(r, r ^ 1) for r in range(N_ROW)]


def _send(x, first, step):
    return lax.ppermute(x, "row", _axis_perm(first, step))


def _swap(x):
    return lax.ppermute(x, "row", SWAP)


def _rep_send(x, k):
    return lax.ppermute(x, "rep", [(i, (i + k) % N_REP) for i in range(N_REP)])


def gather_table(mine):
    line = jnp.concatenate([mine] + [_send(mine, True, k) for k in OFFSETS], axis=0)
    far, near, back = (_send(line, False, k) for k in (2, 1, -1))
    pieces = [line, near, back, far]
    zeros = jnp.zeros((mine.shape[0] // 2, mine.shape[1]), mine.dtype)
    return jnp.concatenate(pieces + [_swap(p) for p in pieces] + [zeros], axis=0)


def table_index(block_index, live):
    me = lax.axis_index("row")
    x, z, c = me // 8, (me // 2) % 4, me % 2
    r = block_index // 8
    dx = (r // 8 - x) % 4
    dz = ((r // 2) % 4 - z) % 4
    cs = r % 2
    rank = lambda d: jnp.where(d == 0, 0, jnp.where(d == 3, 1, jnp.where(d == 1, 2, 3)))
    kx, kz = rank(dx), rank(dz)
    k1 = jnp.where(cs == 0, kx, kz)
    k2 = jnp.where(cs == 0, kz, kx)
    other = (cs != c).astype(jnp.int32)
    pos = ((other * 4 + k2) * 4 + k1) * 2 + (block_index // 4) % 2
    slot = jnp.arange(block_index.shape[1], dtype=jnp.int32)
    return jnp.where(slot < live[:, None], pos, 2 * N_ROW).astype(jnp.int32)


def spmm(index, values, table, member, targets, received=()):
    rb, s, rowb, _ = values.shape
    width = table.shape[1]
    per = rb // N_REP
    n = per * len(targets)

    def kernel(m_ref, idx_ref, v_ref, t_ref, *rest):
        got, outs = rest[: len(received)], rest[len(received) :]
        m = m_ref[0]
        source = [lax.rem(m + targets[i // per], N_REP) * per + i % per for i in range(n)]
        for i in range(n):
            b = source[i]
            acc = jnp.zeros((rowb, width), F32)
            for p in range(0, s, 2):
                lhs = jnp.concatenate([v_ref[b, p], v_ref[b, p + 1]], axis=1)
                rows = [
                    t_ref[pl.ds(pl.multiple_of(idx_ref[b, p + q] * rowb, rowb), rowb), :] for q in range(2)
                ]
                rhs = jnp.concatenate(rows, axis=0)
                acc = acc + jnp.dot(lhs, rhs, preferred_element_type=F32)
            out = outs[i // per]
            rows = pl.ds((i % per) * rowb, rowb)
            if i < per:
                for r in got:
                    acc = acc + r[rows, :].astype(F32)
            out[rows, :] = acc.astype(out.dtype)

    return pl.pallas_call(
        kernel,
        in_specs=[
            pl.BlockSpec(memory_space=pltpu.SMEM),
            pl.BlockSpec(memory_space=pltpu.SMEM),
            pl.BlockSpec(memory_space=pltpu.VMEM),
            pl.BlockSpec(memory_space=pltpu.VMEM),
        ]
        + [pl.BlockSpec(memory_space=pltpu.VMEM)] * len(received),
        out_specs=[pl.BlockSpec(memory_space=pltpu.VMEM)] * len(targets),
        out_shape=[jax.ShapeDtypeStruct((per * rowb, width), F32 if k == 0 else BF16) for k in targets],
        compiler_params=pltpu.CompilerParams(vmem_limit_bytes=4 << 20),
        cost_estimate=pl.CostEstimate(
            flops=n * s * rowb * rowb * width // 8, bytes_accessed=n * rowb * width * 2, transcendentals=0
        ),
    )(member, index, values, table, *received)


def tail(parts, weight, bias, cotangent):
    nodes, width = cotangent.shape

    def kernel(*refs):
        part_refs = refs[: len(parts)]
        w_ref, b_ref, g_ref, out_ref, grad_ref = refs[len(parts) :]
        a = part_refs[0][...].astype(F32)
        for r in part_refs[1:]:
            a = a + r[...].astype(F32)
        a = a.astype(BF16)
        pre = jnp.dot(a, w_ref[...], preferred_element_type=F32)
        pre = pre + b_ref[...]
        sig = jax.nn.sigmoid(pre)
        out_ref[...] = (pre * sig).astype(BF16)
        delta_f = g_ref[...].astype(F32) * sig * (1.0 + pre * (1.0 - sig))
        delta = delta_f.astype(BF16)
        grad_ref[...] = jnp.zeros(grad_ref.shape, BF16)
        bias_row = jnp.sum(delta_f, axis=0, keepdims=True)
        for k in range(4):
            grad_ref[k, pl.ds(16, 8), :] = jnp.broadcast_to(
                bias_row[:, k * 128 : (k + 1) * 128] * 0.125, (8, 128)
            ).astype(BF16)
        g = lax.dot_general(a, delta, (((0,), (0,)), ((), ())), preferred_element_type=F32).astype(BF16)
        for r in range(width // 16):
            for k in range(4):
                grad_ref[r * 4 + k, pl.ds(0, 16), :] = g[r * 16 : (r + 1) * 16, k * 128 : (k + 1) * 128]

    return pl.pallas_call(
        kernel,
        out_shape=[
            jax.ShapeDtypeStruct((nodes, width), BF16),
            jax.ShapeDtypeStruct((128, 24, 128), BF16),
        ],
        compiler_params=pltpu.CompilerParams(vmem_limit_bytes=16 << 20),
    )(*parts, weight, bias.reshape(1, -1), cotangent)


def unpack(packed):
    width = 512

    def kernel(p_ref, grad_ref, bias_ref):
        for r in range(width // 16):
            for k in range(4):
                grad_ref[pl.ds(r * 16, 16), pl.ds(k * 128, 128)] = p_ref[4 * r + k, pl.ds(0, 16), :].astype(F32)
        for k in range(4):
            rows = p_ref[k, pl.ds(16, 8), :].astype(F32)
            bias_ref[:, pl.ds(k * 128, 128)] = jnp.sum(rows, axis=0, keepdims=True)

    return pl.pallas_call(
        kernel,
        out_shape=[jax.ShapeDtypeStruct((width, width), F32), jax.ShapeDtypeStruct((1, width), F32)],
        compiler_params=pltpu.CompilerParams(vmem_limit_bytes=16 << 20),
    )(packed)


def per_device(features, block_index, counts, values, weight, bias, cotangent):
    rb, s = block_index.shape
    rowb = values.shape[2]
    width = features.shape[1]
    member = lax.axis_index("rep")
    live = jnp.clip(counts - member * s, 0, s)
    index = table_index(block_index, live)
    mine = lax.dynamic_index_in_dim(features.reshape(2, N_REP, rowb, width), member, 1, False)
    mine = mine.reshape(2 * rowb, width)
    m_arr = member.astype(jnp.int32).reshape(1)
    table = gather_table(mine)
    (far,) = spmm(index, values, table, m_arr, (2,))
    far = _rep_send(far, 2)
    ahead, behind = spmm(index, values, table, m_arr, (1, 3))
    ahead, behind = _rep_send(ahead, 1), _rep_send(behind, 3)
    (own,) = spmm(index, values, table, m_arr, (0,), (far,))
    parts = [own, ahead, behind]
    output, packed = tail(parts, weight, bias, cotangent)
    got = lax.all_to_all(packed, ("row", "rep"), 0, 0, tiled=False)
    mysum = jnp.sum(got.astype(F32), axis=0).astype(BF16)
    back = lax.all_to_all(jnp.broadcast_to(mysum[None], packed.shape), ("row", "rep"), 0, 0, tiled=False)
    weight_grad, bias_grad = unpack(back)
    bias_grad = bias_grad.reshape(width)
    return (output, weight_grad, bias_grad)


def solution(mesh):
    return jax.shard_map(
        per_device,
        mesh=mesh,
        in_specs=(
            P("row", None),
            P("row", "rep"),
            P("row"),
            P("row", "rep", None, None),
            P(),
            P(),
            P(("row", "rep"), None),
        ),
        out_specs=(P(("row", "rep"), None), P(), P()),
        check_vma=False,
    )
```
